1024 devices in a mesh: rack: 64 (over z, core), local: 16 (over x, y).
Axes of the slice: x: 4, y: 4, z: 32, core: 2. Of those that a mesh axis runs over, the one named last changes fastest.
Arguments:
- x_tokens: bfloat16 [8192, 3584], P('rack', 'local'), may hold values from -6 to 6
- cotangent: bfloat16 [8192, 3584], P('rack', 'local'), may hold values from -4 to 4
- route_probs: bfloat16 [8192, 4], P('rack'), may hold values from 0.099609375 to 1
- expert_ids: int32 [8192, 4], P('rack'), may hold values from 0 to 63, as said below
- w_gate: bfloat16 [64, 3584, 1024], P('rack', 'local'), may hold values from -0.09375 to 0.09375
- w_up: bfloat16 [64, 3584, 1024], P('rack', 'local'), may hold values from -0.09375 to 0.09375
- w_down: bfloat16 [64, 3584, 1024], P('rack', 'local'), may hold values from -0.1875 to 0.1875
Outputs:
- grad_tokens: bfloat16 [8192, 3584], P('rack', 'local')
- grad_probs: float32 [8192, 4], P('rack')
- grad_w_gate: bfloat16 [64, 3584, 1024], P('rack', 'local')
- grad_w_up: bfloat16 [64, 3584, 1024], P('rack', 'local')
- grad_w_down: bfloat16 [64, 3584, 1024], P('rack', 'local')
The draws below stay inside these ranges and needn't reach their ends.
Inputs may be any that keep to these rules, and one draw needn't show every extreme that they name: `expert_ids`: the 4 ids of a token are different. Over the 128 tokens of one rack index each expert is named at most 10 times; half of the experts are named exactly 10 times, and one expert is named 10 times over the tokens of every rack index.
All inputs are finite; a program needn't handle non-finite values.
Results may differ from the reference program's by a relative error of at most 0.03.
Values may be sent and summed in bfloat16 or wider, within the bound.
No kernel may reach another device: no remote copies, remote signals or barrier semaphores. Data moves between devices by JAX's collectives and lax.ppermute only.
A program may use at most 32 MiB of HBM per device.

```python
import math
import jax
import jax.numpy as jnp
from jax import lax

D = 3584
FF = 1024
RACKS_TOKEN = 4
TOK_DEV = 128
TOP = 4
SEND = 10
EXP = 64
TOKENS = 8192
N_RACK = 64
N_LOCAL = 16


def draw_expert_ids(key, part):
    key = jax.random.fold_in(key, 11)
    mean_load = RACKS_TOKEN * TOK_DEV // N_RACK
    spread_load = SEND - mean_load
    key_perm, key_hot, key_tokens, key_slots = jax.random.split(key, 4)
    ordering = jax.vmap(lambda subkey: jax.random.permutation(subkey, N_RACK))(jax.random.split(key_perm, N_RACK))
    rank_of = jnp.argsort(ordering, axis=1).astype(jnp.int32)
    hot_expert = jax.random.randint(key_hot, (), 0, N_RACK)
    hot_rank = rank_of[:, hot_expert]
    expert_col = jnp.arange(N_RACK, dtype=jnp.int32)[None, :]
    rank_of = jnp.where(expert_col == hot_expert, 0, jnp.where(rank_of == 0, hot_rank[:, None], rank_of))
    load_counts = jnp.where(rank_of < N_RACK // 2, mean_load + spread_load, mean_load - spread_load).astype(jnp.int32)
    cumulative = jnp.cumsum(load_counts, axis=1).astype(jnp.int32)
    entries = jnp.arange(RACKS_TOKEN * TOK_DEV, dtype=jnp.int32)
    racks = jax.vmap(lambda bounds: jnp.searchsorted(bounds, entries, side='right'))(cumulative).astype(jnp.int32)
    racks = jnp.transpose(racks.reshape(N_RACK, RACKS_TOKEN, TOK_DEV), (0, 2, 1))
    token_order = jax.vmap(lambda subkey: jax.random.permutation(subkey, TOK_DEV))(jax.random.split(key_tokens, N_RACK))
    racks = jnp.take_along_axis(racks, token_order[:, :, None], axis=1)
    slot_keys = jax.random.split(key_slots, N_RACK * TOK_DEV)
    slot_order = jax.vmap(lambda subkey: jax.random.permutation(subkey, TOP))(slot_keys).reshape(N_RACK, TOK_DEV, TOP)
    racks = jnp.take_along_axis(racks, slot_order, axis=2)
    return racks.reshape(TOKENS, TOP).astype(jnp.int32)


def block_levels(stream_key, extent, cuts, smallest, high):
    def one(axis_at, blocks):
        steps = jax.random.uniform(jax.random.fold_in(jax.random.fold_in(stream_key, 6), axis_at), (blocks,), jnp.float32, smallest / len(cuts), high / len(cuts))
        return jnp.repeat(jnp.exp(steps), extent[axis_at] // blocks).reshape((-1,) + (1,) * (len(extent) - axis_at - 1))

    factor_of = one(*cuts[0])
    for cut in cuts[1:]:
        factor_of = factor_of * one(*cut)
    return factor_of


def centred(rng, shape, scale, limit, cuts=(), held_as=jnp.bfloat16):
    array = jax.random.normal(rng, shape, jnp.float32) * scale
    if len(cuts) > 0:
        array = block_levels(rng, shape, cuts, -0.22, 0.18) * array
    return jnp.clip(array, min=-limit, max=limit).astype(held_as)


def setup_inputs(seed: int = 0) -> dict:
    key_list = jax.random.split(jax.random.key(seed), 8)
    x_tokens = centred(key_list[0], (TOKENS, D), 1.0, 6.0, ((0, 64), (1, 16)))
    cotangent = centred(key_list[1], (TOKENS, D), 0.5, 4.0, ((0, 64), (1, 16)))
    route_probs = jnp.clip(jnp.exp(math.log(1.0) - 2.306499 * jax.random.uniform(key_list[2], (TOKENS, TOP), jnp.float32) ** block_levels(key_list[2], (TOKENS, TOP), ((0, 64),), -0.2, 0.2)), 0.099609375, 1.0).astype(jnp.bfloat16)
    expert_ids = draw_expert_ids(jax.random.fold_in(key_list[7], 71), 0)
    w_gate = centred(key_list[4], (EXP, D, FF), D ** -0.5, 0.09375, ((0, 64), (1, 16)))
    w_up = centred(key_list[5], (EXP, D, FF), D ** -0.5, 0.09375, ((0, 64), (1, 16)))
    w_down = centred(key_list[6], (EXP, D, FF), FF ** -0.5, 0.1875, ((0, 64), (1, 16)))
    return dict(x_tokens=x_tokens, cotangent=cotangent, route_probs=route_probs, expert_ids=expert_ids, w_gate=w_gate, w_up=w_up, w_down=w_down)


def reference(x_tokens, cotangent, route_probs, expert_ids, w_gate, w_up, w_down):
    row_total = N_RACK * SEND
    slice_width = D // N_LOCAL
    probs_full = route_probs.astype(jnp.float32)
    highest = lax.Precision.HIGHEST

    def summed(operand, weight):
        pieces = jnp.einsum("rjd,jdf->rjf", operand, weight.reshape(N_LOCAL, slice_width, FF))
        pieces = lax.optimization_barrier(pieces.astype(jnp.bfloat16)).astype(jnp.float32)
        return jnp.sum(pieces, axis=1)

    def one_expert(running, inputs):
        expert_num, weight_gate, weight_up, weight_down = inputs
        matched = expert_ids == expert_num
        in_use = jnp.any(matched, axis=1)
        row_index = jnp.nonzero(in_use, size=row_total, fill_value=0)[0].astype(jnp.int32)
        present = (jnp.arange(row_total, dtype=jnp.int32) < jnp.sum(in_use.astype(jnp.int32))).astype(jnp.float32)
        rows_x = x_tokens[row_index].astype(jnp.float32) * present[:, None]
        rows_dy = cotangent[row_index].astype(jnp.float32) * present[:, None]
        row_matched = matched[row_index]
        rows_p = jnp.sum(jnp.where(row_matched, probs_full[row_index], 0.0), axis=1) * present
        gate_f = weight_gate.astype(jnp.float32)
        up_f = weight_up.astype(jnp.float32)
        down_f = weight_down.astype(jnp.float32)
        piece_x = rows_x.reshape(row_total, N_LOCAL, slice_width)
        piece_dy = rows_dy.reshape(row_total, N_LOCAL, slice_width)
        gate_pre = summed(piece_x, gate_f)
        up_pre = summed(piece_x, up_f)
        back_proj = summed(piece_dy, down_f)
        logistic = jax.nn.sigmoid(gate_pre)
        active = gate_pre * logistic
        slope = logistic * (1.0 + gate_pre * (1.0 - logistic))
        hidden = active * up_pre
        statistic = lax.optimization_barrier(jnp.sum(hidden * back_proj, axis=1).astype(jnp.bfloat16)).astype(jnp.float32)
        scaled = lax.optimization_barrier((rows_p[:, None] * hidden).astype(jnp.bfloat16)).astype(jnp.float32)
        grad_hidden = rows_p[:, None] * back_proj
        grad_up = lax.optimization_barrier((grad_hidden * active).astype(jnp.bfloat16)).astype(jnp.float32)
        grad_gate = lax.optimization_barrier((grad_hidden * up_pre * slope).astype(jnp.bfloat16)).astype(jnp.float32)
        term = jnp.dot(grad_gate, gate_f.T, precision=highest) + jnp.dot(grad_up, up_f.T, precision=highest)
        term = lax.optimization_barrier(term.astype(jnp.bfloat16)).astype(jnp.float32)
        grad_g = jnp.dot(rows_x.T, grad_gate, precision=highest).astype(jnp.bfloat16)
        grad_u = jnp.dot(rows_x.T, grad_up, precision=highest).astype(jnp.bfloat16)
        grad_d = jnp.dot(rows_dy.T, scaled, precision=highest).astype(jnp.bfloat16)
        dx_total, prob_total = running
        dx_total = dx_total.at[row_index].add(term * present[:, None])
        prob_terms = jnp.where(row_matched, statistic[:, None], 0.0) * present[:, None]
        prob_total = prob_total.at[row_index].add(prob_terms)
        return (dx_total, prob_total), (grad_g, grad_u, grad_d)

    start_state = (jnp.zeros((TOKENS, D), jnp.float32), jnp.zeros((TOKENS, TOP), jnp.float32))
    expert_numbers = jnp.arange(EXP, dtype=jnp.int32)
    (dx_total, prob_total), (grad_w_gate, grad_w_up, grad_w_down) = lax.scan(
        one_expert, start_state, (expert_numbers, w_gate, w_up, w_down))
    return dx_total.astype(jnp.bfloat16), prob_total, grad_w_gate, grad_w_up, grad_w_down
```

```python
import jax
import jax.numpy as jnp
from jax import lax
from jax.sharding import PartitionSpec as P

RACKS_TOKEN = 4
LANES = 128


def activate(gate_pre, up_pre, back_proj, weights):
    logistic = jax.nn.sigmoid(gate_pre)
    active = gate_pre * logistic
    slope = logistic * (1.0 + gate_pre * (1.0 - logistic))
    hidden = active * up_pre
    statistic = jnp.sum(hidden * back_proj, axis=1)
    grad_hidden = weights[:, None] * back_proj
    grad_gate = (grad_hidden * up_pre * slope).astype(jnp.bfloat16)
    grad_up = (grad_hidden * active).astype(jnp.bfloat16)
    scaled = (weights[:, None] * hidden).astype(jnp.bfloat16)
    return (grad_gate, grad_up, scaled, statistic)


def exchange(rows, axis):
    return lax.all_to_all(rows, axis, split_axis=0, concat_axis=0, tiled=True)


def local(x_tokens, cotangent, route_probs, expert_ids, w_gate, w_up, w_down):
    tok_count, width = x_tokens.shape
    rack_count = lax.axis_size("rack")
    local_count = lax.axis_size("local")
    send_rows = 5 * RACKS_TOKEN * tok_count // (4 * rack_count)
    row_total = rack_count * send_rows
    own_rows = row_total // local_count
    chunks = width // LANES + 1
    padded = chunks * LANES
    weight_gate, weight_up, weight_down = w_gate[0], w_up[0], w_down[0]
    hidden_units = weight_gate.shape[1]

    rack_ids = jnp.arange(rack_count, dtype=jnp.int32)
    member = expert_ids[:, :, None] == rack_ids[None, None, :]
    in_use = jnp.any(member, axis=1)
    slot_rank = jnp.cumsum(in_use.astype(jnp.int32), axis=0) - 1
    slot_ids = jnp.arange(send_rows, dtype=jnp.int32)
    selector = in_use.T[:, None, :] & (slot_rank.T[:, None, :] == slot_ids[None, :, None])
    selector_bf = selector.astype(jnp.bfloat16)

    def pack(rows, extra):
        filled = jnp.concatenate(
            [rows, extra[..., None], jnp.zeros(rows.shape[:-1] + (padded - width - 1,), rows.dtype)], axis=-1
        )
        return filled.reshape(rack_count, send_rows, chunks, LANES)

    def picked(tokens):
        return jnp.einsum("rst,td->rsd", selector_bf, tokens, preferred_element_type=jnp.float32).astype(jnp.bfloat16)

    prob_rack = jnp.sum(jnp.where(member, route_probs.astype(jnp.float32)[:, :, None], 0.0), axis=1)
    send_prob = jnp.sum(jnp.where(selector, prob_rack.T[:, None, :], 0.0), axis=2).astype(jnp.bfloat16)

    came_x = exchange(pack(picked(x_tokens), jnp.zeros_like(send_prob)), "rack")
    send_dy = pack(picked(cotangent), send_prob)
    came_x, send_dy = lax.optimization_barrier((came_x, send_dy))
    came_dy = exchange(send_dy, "rack")

    rows_x = came_x.reshape(row_total, padded)[:, :width]
    partial = jnp.concatenate(
        [
            jnp.dot(rows_x, weight_gate, preferred_element_type=jnp.float32).astype(jnp.bfloat16),
            jnp.dot(rows_x, weight_up, preferred_element_type=jnp.float32).astype(jnp.bfloat16),
        ],
        axis=1,
    )
    own_pre = lax.psum_scatter(partial, "local", scatter_dimension=0, tiled=True).astype(jnp.float32)

    full_dy = came_dy.reshape(row_total, padded)
    rows_dy = full_dy[:, :width]
    rows_prob = full_dy[:, width].astype(jnp.float32)
    back = jnp.dot(rows_dy, weight_down, preferred_element_type=jnp.float32).astype(jnp.bfloat16)
    back_parts = exchange(back.reshape(local_count, own_rows, hidden_units), "local")
    own_back = jnp.sum(back_parts.astype(jnp.float32), axis=0)

    own_first = lax.axis_index("local") * own_rows
    own_prob = lax.dynamic_slice_in_dim(rows_prob, own_first, own_rows, 0)
    grad_gate, grad_up, scaled, statistic = activate(
        own_pre[:, :hidden_units], own_pre[:, hidden_units:], own_back, own_prob
    )
    stat_lanes = jnp.broadcast_to(statistic.astype(jnp.bfloat16)[:, None], (own_rows, LANES))
    packed = jnp.concatenate([grad_gate, grad_up, stat_lanes], axis=1)
    grads_in = exchange(jnp.broadcast_to(packed[None], (local_count,) + packed.shape), "local")
    grads_in = grads_in.reshape(row_total, 2 * hidden_units + LANES)
    scaled, grads_in = lax.optimization_barrier((scaled, grads_in))
    scaled_in = lax.all_gather(scaled, "local", axis=0, tiled=True)

    gate_in = grads_in[:, :hidden_units]
    up_in = grads_in[:, hidden_units : 2 * hidden_units]
    stats_in = grads_in[:, 2 * hidden_units]
    contract_units = (((1,), (1,)), ((), ()))
    contract_rows = (((0,), (0,)), ((), ()))
    term = lax.dot_general(gate_in, weight_gate, contract_units, preferred_element_type=jnp.float32)
    term = term + lax.dot_general(up_in, weight_up, contract_units, preferred_element_type=jnp.float32)
    back_terms = pack(
        term.astype(jnp.bfloat16).reshape(rack_count, send_rows, width), stats_in.reshape(rack_count, send_rows)
    )
    came_terms = exchange(back_terms, "rack").reshape(rack_count, send_rows, padded)

    grad_g = lax.dot_general(rows_x, gate_in, contract_rows, preferred_element_type=jnp.float32)
    grad_u = lax.dot_general(rows_x, up_in, contract_rows, preferred_element_type=jnp.float32)
    grad_d = lax.dot_general(rows_dy, scaled_in, contract_rows, preferred_element_type=jnp.float32)

    grad_tokens = jnp.einsum(
        "rst,rsd->td", selector_bf, came_terms[..., :width], preferred_element_type=jnp.float32
    ).astype(jnp.bfloat16)
    came_stat = came_terms[..., width].astype(jnp.float32)
    stat_token = jnp.sum(jnp.where(selector, came_stat[:, :, None], 0.0), axis=1)
    grad_probs = jnp.sum(jnp.where(member, stat_token.T[:, None, :], 0.0), axis=2)
    return (
        grad_tokens,
        grad_probs,
        grad_g.astype(jnp.bfloat16)[None],
        grad_u.astype(jnp.bfloat16)[None],
        grad_d.astype(jnp.bfloat16)[None],
    )


def solution(mesh):
    placed = (
        P("rack", "local"),
        P("rack", "local"),
        P("rack", None),
        P("rack", None),
        P("rack", "local", None),
        P("rack", "local", None),
        P("rack", "local", None),
    )
    return jax.shard_map(
        local,
        mesh=mesh,
        in_specs=placed,
        out_specs=(
            P("rack", "local"),
            P("rack", None),
            P("rack", "local", None),
            P("rack", "local", None),
            P("rack", "local", None),
        ),
        check_vma=False,
    )
```

```python
import jax
import jax.numpy as jnp
from jax import lax
from jax.sharding import PartitionSpec as P

RACKS_TOKEN = 4
LANES = 128
PAIR = 2


def activate(gate_pre, up_pre, back_proj, weights):
    logistic = jax.nn.sigmoid(gate_pre)
    active = gate_pre * logistic
    slope = logistic * (1.0 + gate_pre * (1.0 - logistic))
    hidden = active * up_pre
    statistic = jnp.sum(hidden * back_proj, axis=1)
    grad_hidden = weights[:, None] * back_proj
    grad_gate = (grad_hidden * up_pre * slope).astype(jnp.bfloat16)
    grad_up = (grad_hidden * active).astype(jnp.bfloat16)
    scaled = (weights[:, None] * hidden).astype(jnp.bfloat16)
    return (grad_gate, grad_up, scaled, statistic)


def exchange(rows, axis, groups=None):
    return lax.all_to_all(rows, axis, split_axis=0, concat_axis=0, tiled=True, axis_index_groups=groups)


def local(x_tokens, cotangent, route_probs, expert_ids, w_gate, w_up, w_down):
    tok_count, width = x_tokens.shape
    rack_count = lax.axis_size("rack")
    local_count = lax.axis_size("local")
    team = local_count // PAIR
    teams = [[PAIR * q + c for q in range(team)] for c in range(PAIR)]
    partners = [(i, i ^ 1) for i in range(local_count)]
    place = lax.axis_index("local")
    slots = 5 * RACKS_TOKEN * tok_count // (4 * rack_count) // PAIR
    row_total = rack_count * slots
    own_rows = row_total // team
    hidden_units = w_gate.shape[2]
    wide = PAIR * width

    own = jnp.concatenate([x_tokens, cotangent], axis=1)
    other = lax.ppermute(own, "local", partners)
    tokens = jnp.concatenate([x_tokens, other[:, :width], cotangent, other[:, width:]], axis=1)
    own_weights = jnp.concatenate([w_gate[0], w_up[0], w_down[0]], axis=1)
    own_weights, tokens = lax.optimization_barrier((own_weights, tokens))
    other_weights = lax.ppermute(own_weights, "local", partners)

    rack_ids = jnp.arange(rack_count, dtype=jnp.int32)
    member = expert_ids[:, :, None] == rack_ids[None, None, :]
    in_use = jnp.any(member, axis=1)
    slot_rank = jnp.cumsum(in_use.astype(jnp.int32), axis=0) - 1
    slot_ids = jnp.arange(slots, dtype=jnp.int32) + (place % PAIR) * slots
    selector = in_use.T[None, :, :] & (slot_rank.T[None, :, :] == slot_ids[:, None, None])
    selector_bf = selector.astype(jnp.bfloat16)
    prob_rack = jnp.sum(jnp.where(member, route_probs.astype(jnp.float32)[:, :, None], 0.0), axis=1)
    send_prob = jnp.sum(jnp.where(selector, prob_rack.T[None, :, :], 0.0), axis=2).astype(jnp.bfloat16)

    chunks = PAIR * wide // LANES
    picked = [
        jnp.einsum(
            "srt,td->srd", selector_bf, tokens[:, k * LANES : (k + 1) * LANES], preferred_element_type=jnp.float32
        ).astype(jnp.bfloat16)
        for k in range(chunks)
    ]
    picked.append(jnp.pad(send_prob.T, ((0, 0), (0, LANES - slots)))[None])
    message = jnp.concatenate(picked, axis=0)
    message_rows = message.shape[0]
    came = exchange(message.transpose(1, 0, 2).reshape(rack_count, message_rows // 2, 2, LANES), "rack")
    came = came.reshape(rack_count, message_rows, LANES).transpose(1, 0, 2)
    rows_both = jnp.concatenate(
        [came[k * slots : (k + 1) * slots].reshape(row_total, LANES) for k in range(chunks)], axis=1
    )
    rows_x, rows_dy = rows_both[:, :wide], rows_both[:, wide:]
    rows_prob = came[message_rows - 1, :, :slots].T.reshape(row_total).astype(jnp.float32)

    weights = jnp.concatenate([own_weights, other_weights], axis=0)
    weight_gu, weight_down = weights[:, : 2 * hidden_units], weights[:, 2 * hidden_units :]
    partial = jnp.concatenate(
        [
            jnp.dot(rows_x, weight_gu, preferred_element_type=jnp.float32).astype(jnp.bfloat16),
            jnp.dot(rows_dy, weight_down, preferred_element_type=jnp.float32).astype(jnp.bfloat16),
        ],
        axis=1,
    )
    parts = exchange(partial.reshape(team, own_rows, 3 * hidden_units), "local", teams)
    sums = jnp.sum(parts.astype(jnp.float32), axis=0)

    own_prob = lax.dynamic_slice_in_dim(rows_prob, (place // PAIR) * own_rows, own_rows, 0)
    grad_gate, grad_up, scaled, statistic = activate(
        sums[:, :hidden_units], sums[:, hidden_units : 2 * hidden_units], sums[:, 2 * hidden_units :], own_prob
    )
    stat_lanes = jnp.broadcast_to(statistic.astype(jnp.bfloat16)[:, None], (own_rows, LANES))
    packed = jnp.concatenate([grad_gate, grad_up, scaled, stat_lanes], axis=1)
    grads_in = exchange(jnp.broadcast_to(packed[None], (team,) + packed.shape), "local", teams)
    grads_in = grads_in.reshape(row_total, 3 * hidden_units + LANES)
    gate_up_in = grads_in[:, : 2 * hidden_units]
    scaled_in = grads_in[:, 2 * hidden_units : 3 * hidden_units]
    stats_in = grads_in[:, 3 * hidden_units : 3 * hidden_units + 1]

    term = lax.dot_general(
        gate_up_in, weight_gu, (((1,), (1,)), ((), ())), preferred_element_type=jnp.float32
    ).astype(jnp.bfloat16)
    back_chunks = wide // LANES + 1
    spare = back_chunks * LANES - wide
    back = jnp.concatenate([term, jnp.broadcast_to(stats_in, (row_total, spare))], axis=1)
    back = back.reshape(slots, rack_count, back_chunks, LANES).transpose(1, 0, 2, 3)
    came_terms = exchange(back, "rack").reshape(rack_count, slots, back_chunks * LANES)

    contract_rows = (((0,), (0,)), ((), ()))

    def outer(first):
        return jnp.concatenate(
            [
                lax.dot_general(
                    rows_x[:, first : first + width], gate_up_in, contract_rows, preferred_element_type=jnp.float32
                ),
                lax.dot_general(
                    rows_dy[:, first : first + width], scaled_in, contract_rows, preferred_element_type=jnp.float32
                ),
            ],
            axis=1,
        )

    came_grads = lax.ppermute(outer(width).astype(jnp.bfloat16), "local", partners)
    grads = (outer(0) + came_grads.astype(jnp.float32)).astype(jnp.bfloat16)

    token_sums = jnp.einsum("srt,rsd->td", selector_bf, came_terms[..., :wide], preferred_element_type=jnp.float32)
    came_stat = came_terms[..., wide].astype(jnp.float32).T
    stat_token = jnp.sum(jnp.where(selector, came_stat[:, :, None], 0.0), axis=0)
    prob_sums = jnp.sum(jnp.where(member, stat_token.T[:, None, :], 0.0), axis=2)
    tail = jnp.concatenate([token_sums[:, width:], prob_sums], axis=1).astype(jnp.bfloat16)
    came_tail = lax.ppermute(tail, "local", partners).astype(jnp.float32)
    grad_tokens = (token_sums[:, :width] + came_tail[:, :width]).astype(jnp.bfloat16)
    grad_probs = prob_sums + came_tail[:, width:]
    return (
        grad_tokens,
        grad_probs,
        grads[None, :, :hidden_units],
        grads[None, :, hidden_units : 2 * hidden_units],
        grads[None, :, 2 * hidden_units :],
    )


def solution(mesh):
    placed = (
        P("rack", "local"),
        P("rack", "local"),
        P("rack", None),
        P("rack", None),
        P("rack", "local", None),
        P("rack", "local", None),
        P("rack", "local", None),
    )
    return jax.shard_map(
        local,
        mesh=mesh,
        in_specs=placed,
        out_specs=(
            P("rack", "local"),
            P("rack", None),
            P("rack", "local", None),
            P("rack", "local", None),
            P("rack", "local", None),
        ),
        check_vma=False,
    )
```

```python
import jax
import jax.numpy as jnp
from jax import lax
from jax.sharding import PartitionSpec as P

RACKS_TOKEN = 4
LANES = 128
PAIR = 2
SIDE = 4


def activate(gate_pre, up_pre, back_proj, weights):
    logistic = jax.nn.sigmoid(gate_pre)
    active = gate_pre * logistic
    slope = logistic * (1.0 + gate_pre * (1.0 - logistic))
    hidden = active * up_pre
    statistic = jnp.sum(hidden * back_proj, axis=1)
    grad_hidden = weights[:, None] * back_proj
    grad_gate = (grad_hidden * up_pre * slope).astype(jnp.bfloat16)
    grad_up = (grad_hidden * active).astype(jnp.bfloat16)
    scaled = (weights[:, None] * hidden).astype(jnp.bfloat16)
    return (grad_gate, grad_up, scaled, statistic)


def exchange(rows, axis, groups=None):
    return lax.all_to_all(rows, axis, split_axis=0, concat_axis=0, tiled=True, axis_index_groups=groups)


def local(x_tokens, cotangent, route_probs, expert_ids, w_gate, w_up, w_down):
    tok_count, width = x_tokens.shape
    rack_count = lax.axis_size("rack")
    local_count = lax.axis_size("local")
    team = local_count // PAIR
    teams = [[i for i in range(local_count) if (i % SIDE + 1) // 2 % PAIR == c] for c in range(PAIR)]
    partners = [(i, i ^ 1) for i in range(local_count)]
    place = lax.axis_index("local")
    slots = 5 * RACKS_TOKEN * tok_count // (4 * rack_count) // PAIR
    row_total = rack_count * slots
    own_rows = row_total // team
    hidden_units = w_gate.shape[2]
    wide = PAIR * width

    x_cols, dy_cols = x_tokens.T, cotangent.T
    other = lax.ppermute(jnp.concatenate([x_cols, dy_cols], axis=0), "local", partners)
    tokens = jnp.concatenate([x_cols, other[:width], dy_cols, other[width:]], axis=0)

    rack_ids = jnp.arange(rack_count, dtype=jnp.int32)
    member = expert_ids[:, :, None] == rack_ids[None, None, :]
    in_use = jnp.any(member, axis=1)
    slot_rank = jnp.cumsum(in_use.astype(jnp.int32), axis=0) - 1
    slot_ids = jnp.arange(slots, dtype=jnp.int32) + (place % SIDE + 1) // 2 % PAIR * slots
    selector = in_use.T[None, :, :] & (slot_rank.T[None, :, :] == slot_ids[:, None, None])
    selector_bf = selector.astype(jnp.bfloat16)
    prob_rack = jnp.sum(jnp.where(member, route_probs.astype(jnp.float32)[:, :, None], 0.0), axis=1)
    send_prob = jnp.sum(jnp.where(selector, prob_rack.T[None, :, :], 0.0), axis=2).astype(jnp.bfloat16)

    chunks = PAIR * wide // LANES
    picked = [
        jnp.einsum(
            "srt,dt->srd", selector_bf, tokens[k * LANES : (k + 1) * LANES], preferred_element_type=jnp.float32
        ).astype(jnp.bfloat16)
        for k in range(chunks)
    ]
    picked.append(jnp.pad(send_prob.T, ((0, 0), (0, LANES - slots)))[None])
    message = jnp.concatenate(picked, axis=0)
    message_rows = message.shape[0]
    message = message.transpose(1, 0, 2).reshape(rack_count, message_rows // 2, 2, LANES)
    message, w_gate, w_up, w_down = lax.optimization_barrier((message, w_gate, w_up, w_down))
    came = exchange(message, "rack")
    came = came.reshape(rack_count, message_rows, LANES).transpose(1, 0, 2)
    rows_both = jnp.concatenate(
        [came[k * slots : (k + 1) * slots].reshape(row_total, LANES) for k in range(chunks)], axis=1
    )
    rows_prob = came[message_rows - 1, :, :slots].T.reshape(row_total).astype(jnp.float32)

    own_weights = jnp.concatenate([w_gate[0], w_up[0], w_down[0]], axis=1)
    other_weights = lax.ppermute(own_weights, "local", partners)
    weights = jnp.concatenate([own_weights, other_weights], axis=0)
    weight_gu, weight_down = weights[:, : 2 * hidden_units], weights[:, 2 * hidden_units :]
    blocks = lax.optimization_barrier(
        jnp.concatenate(
            [
                jnp.pad(weight_gu, ((0, 0), (0, hidden_units))),
                jnp.pad(weight_down, ((0, 0), (2 * hidden_units, 0))),
            ],
            axis=0,
        )
    )
    partial = jnp.dot(rows_both, blocks, preferred_element_type=jnp.float32).astype(jnp.bfloat16)
    parts = exchange(partial.reshape(team, own_rows, 3 * hidden_units), "local", teams)
    sums = jnp.sum(parts.astype(jnp.float32), axis=0)

    own_prob = lax.dynamic_slice_in_dim(rows_prob, place // PAIR * own_rows, own_rows, 0)
    grad_gate, grad_up, scaled, statistic = activate(
        sums[:, :hidden_units], sums[:, hidden_units : 2 * hidden_units], sums[:, 2 * hidden_units :], own_prob
    )
    stat_lanes = jnp.broadcast_to(statistic.astype(jnp.bfloat16)[:, None], (own_rows, LANES))
    packed = jnp.concatenate([grad_gate, grad_up, scaled, stat_lanes], axis=1)
    grads_in = exchange(jnp.broadcast_to(packed[None], (team,) + packed.shape), "local", teams)
    grads_in = grads_in.reshape(row_total, 3 * hidden_units + LANES)
    stats_in = grads_in[:, 3 * hidden_units : 3 * hidden_units + 1]

    term = lax.dot_general(
        grads_in[:, : 2 * hidden_units], blocks[:wide, : 2 * hidden_units], (((1,), (1,)), ((), ())), preferred_element_type=jnp.float32
    ).astype(jnp.bfloat16)
    back_chunks = wide // LANES + 1
    spare = back_chunks * LANES - wide
    back = jnp.concatenate([term, jnp.broadcast_to(stats_in, (row_total, spare))], axis=1)
    back = back.reshape(slots, rack_count, back_chunks, LANES).transpose(1, 0, 2, 3)
    back, rows_both, grads_in = lax.optimization_barrier((back, rows_both, grads_in))
    came_terms = exchange(back, "rack").reshape(rack_count, slots, back_chunks * LANES)

    contract_rows = (((0,), (0,)), ((), ()))
    rows_x, rows_dy = rows_both[:, :wide], rows_both[:, wide:]
    gate_up_in = grads_in[:, : 2 * hidden_units]
    scaled_in = grads_in[:, 2 * hidden_units : 3 * hidden_units]

    def outer(first):
        return jnp.concatenate(
            [
                lax.dot_general(
                    rows_x[:, first : first + width], gate_up_in, contract_rows, preferred_element_type=jnp.float32
                ),
                lax.dot_general(
                    rows_dy[:, first : first + width], scaled_in, contract_rows, preferred_element_type=jnp.float32
                ),
            ],
            axis=1,
        )

    came_grads = lax.ppermute(outer(width).astype(jnp.bfloat16), "local", partners)
    grads = (outer(0) + came_grads.astype(jnp.float32)).astype(jnp.bfloat16)

    token_sums = jnp.einsum("srt,rsd->td", selector_bf, came_terms[..., :wide], preferred_element_type=jnp.float32)
    came_stat = came_terms[..., wide].astype(jnp.float32).T
    stat_token = jnp.sum(jnp.where(selector, came_stat[:, :, None], 0.0), axis=0)
    prob_sums = jnp.sum(jnp.where(member, stat_token.T[:, None, :], 0.0), axis=2)
    tail = jnp.concatenate([token_sums[:, width:], prob_sums], axis=1).astype(jnp.bfloat16)
    came_tail = lax.ppermute(tail, "local", partners).astype(jnp.float32)
    grad_tokens = (token_sums[:, :width] + came_tail[:, :width]).astype(jnp.bfloat16)
    grad_probs = prob_sums + came_tail[:, width:]
    return (
        grad_tokens,
        grad_probs,
        grads[None, :, :hidden_units],
        grads[None, :, hidden_units : 2 * hidden_units],
        grads[None, :, 2 * hidden_units :],
    )


def solution(mesh):
    placed = (
        P("rack", "local"),
        P("rack", "local"),
        P("rack", None),
        P("rack", None),
        P("rack", "local", None),
        P("rack", "local", None),
        P("rack", "local", None),
    )
    return jax.shard_map(
        local,
        mesh=mesh,
        in_specs=placed,
        out_specs=(
            P("rack", "local"),
            P("rack", None),
            P("rack", "local", None),
            P("rack", "local", None),
            P("rack", "local", None),
        ),
        check_vma=False,
    )
```

```python
import jax
import jax.numpy as jnp
from jax import lax
from jax.experimental import pallas as pl
from jax.sharding import PartitionSpec as P

RACKS_TOKEN = 4
LANES = 128
PAIR = 2
SIDE = 4


def activate(gate_pre, up_pre, back_proj, weights):
    logistic = jax.nn.sigmoid(gate_pre)
    active = gate_pre * logistic
    slope = logistic * (1.0 + gate_pre * (1.0 - logistic))
    hidden = active * up_pre
    statistic = jnp.sum(hidden * back_proj, axis=1)
    grad_hidden = weights[:, None] * back_proj
    grad_gate = (grad_hidden * up_pre * slope).astype(jnp.bfloat16)
    grad_up = (grad_hidden * active).astype(jnp.bfloat16)
    scaled = (weights[:, None] * hidden).astype(jnp.bfloat16)
    return (grad_gate, grad_up, scaled, statistic)


def exchange(rows, axis, groups=None):
    return lax.all_to_all(rows, axis, split_axis=0, concat_axis=0, tiled=True, axis_index_groups=groups)


def project(rows, weights, gate_up):
    count, lanes = rows.shape
    depth, columns = weights.shape
    tile = 4 * LANES

    def kernel(rows_ref, weights_ref, out_ref):
        first = jnp.where(pl.program_id(0) < gate_up // tile, 0, (lanes - depth) // LANES)
        window = rows_ref[:, pl.ds(pl.multiple_of(first * LANES, LANES), depth)]
        out_ref[...] = jnp.dot(window, weights_ref[...], preferred_element_type=jnp.float32).astype(out_ref.dtype)

    return pl.pallas_call(
        kernel,
        grid=(columns // tile,),
        in_specs=[
            pl.BlockSpec((count, lanes), lambda n: (0, 0)),
            pl.BlockSpec((depth, tile), lambda n: (0, n)),
        ],
        out_specs=pl.BlockSpec((count, tile), lambda n: (0, n)),
        out_shape=jax.ShapeDtypeStruct((count, columns), rows.dtype),
        cost_estimate=pl.CostEstimate(
            flops=2 * count * depth * columns,
            bytes_accessed=2 * (count * lanes + depth * columns + count * columns),
            transcendentals=0,
        ),
    )(rows, weights)


def local(x_tokens, cotangent, route_probs, expert_ids, w_gate, w_up, w_down):
    tok_count, width = x_tokens.shape
    rack_count = lax.axis_size("rack")
    local_count = lax.axis_size("local")
    team = local_count // PAIR
    teams = [[i for i in range(local_count) if (i % SIDE + 1) // 2 % PAIR == c] for c in range(PAIR)]
    partners = [(i, i ^ 1) for i in range(local_count)]
    place = lax.axis_index("local")
    slots = 5 * RACKS_TOKEN * tok_count // (4 * rack_count) // PAIR
    row_total = rack_count * slots
    own_rows = row_total // team
    hidden_units = w_gate.shape[2]
    wide = PAIR * width

    x_cols, dy_cols = x_tokens.T, cotangent.T
    own = jnp.concatenate([x_cols, dy_cols], axis=0)
    other = lax.ppermute(own, "local", partners)
    tokens = lax.optimization_barrier(
        jnp.concatenate([own[:width], other[:width], own[width:], other[width:]], axis=0)
    )

    rack_ids = jnp.arange(rack_count, dtype=jnp.int32)
    member = expert_ids[:, :, None] == rack_ids[None, None, :]
    in_use = jnp.any(member, axis=1)
    slot_rank = jnp.cumsum(in_use.astype(jnp.int32), axis=0) - 1
    slot_ids = jnp.arange(slots, dtype=jnp.int32) + (place % SIDE + 1) // 2 % PAIR * slots
    selector = in_use.T[None, :, :] & (slot_rank.T[None, :, :] == slot_ids[:, None, None])
    selector_bf = selector.astype(jnp.bfloat16)
    prob_rack = jnp.sum(jnp.where(member, route_probs.astype(jnp.float32)[:, :, None], 0.0), axis=1)
    send_prob = jnp.sum(jnp.where(selector, prob_rack.T[None, :, :], 0.0), axis=2).astype(jnp.bfloat16)

    chunks = PAIR * wide // LANES
    picked = [
        jnp.einsum(
            "srt,dt->srd", selector_bf, tokens[k * LANES : (k + 1) * LANES], preferred_element_type=jnp.float32
        ).astype(jnp.bfloat16)
        for k in range(chunks)
    ]
    picked.append(jnp.pad(send_prob.T, ((0, 0), (0, LANES - slots)))[None])
    message = jnp.concatenate(picked, axis=0)
    message_rows = message.shape[0]
    message = message.transpose(1, 0, 2).reshape(rack_count, message_rows // 2, 2, LANES)
    message, w_gate, w_up, w_down = lax.optimization_barrier((message, w_gate, w_up, w_down))
    came = exchange(message, "rack")
    came = came.reshape(rack_count, message_rows, LANES).transpose(1, 0, 2)
    rows_both = jnp.concatenate(
        [came[k * slots : (k + 1) * slots].reshape(row_total, LANES) for k in range(chunks)], axis=1
    )
    rows_prob = came[message_rows - 1, :, :slots].T.reshape(row_total).astype(jnp.float32)

    own_weights = jnp.concatenate([w_gate[0], w_up[0], w_down[0]], axis=1)
    other_weights = lax.ppermute(own_weights, "local", partners)
    weights = jnp.concatenate([own_weights, other_weights], axis=0)
    weight_gu, weight_down = weights[:, : 2 * hidden_units], weights[:, 2 * hidden_units :]
    depth = (wide + LANES - 1) // LANES * LANES
    filled = lax.optimization_barrier(
        jnp.concatenate(
            [
                jnp.pad(weight_gu, ((0, depth - wide), (0, 0))),
                jnp.pad(weight_down, ((depth - wide, 0), (0, 0))),
            ],
            axis=1,
        )
    )
    partial = project(rows_both, filled, 2 * hidden_units)
    parts = exchange(partial.reshape(team, own_rows, 3 * hidden_units), "local", teams)
    sums = jnp.sum(parts.astype(jnp.float32), axis=0)

    own_prob = lax.dynamic_slice_in_dim(rows_prob, place // PAIR * own_rows, own_rows, 0)
    grad_gate, grad_up, scaled, statistic = activate(
        sums[:, :hidden_units], sums[:, hidden_units : 2 * hidden_units], sums[:, 2 * hidden_units :], own_prob
    )
    stat_lanes = jnp.broadcast_to(statistic.astype(jnp.bfloat16)[:, None], (own_rows, LANES))
    packed = jnp.concatenate([grad_gate, grad_up, stat_lanes], axis=1)
    grads_in = exchange(jnp.broadcast_to(packed[None], (team,) + packed.shape), "local", teams)
    grads_in = grads_in.reshape(row_total, 2 * hidden_units + LANES)
    stats_in = grads_in[:, 2 * hidden_units : 2 * hidden_units + 1]

    term = lax.dot_general(
        grads_in[:, : 2 * hidden_units],
        filled[:, : 2 * hidden_units],
        (((1,), (1,)), ((), ())),
        preferred_element_type=jnp.float32,
    ).astype(jnp.bfloat16)
    back = jnp.where(jnp.arange(depth)[None, :] < wide, term, stats_in)
    back = back.reshape(slots, rack_count, depth // LANES, LANES).transpose(1, 0, 2, 3)
    back, rows_both, grads_in, scaled = lax.optimization_barrier((back, rows_both, grads_in, scaled))
    came_terms = exchange(back, "rack").reshape(rack_count, slots, depth)

    around = [
        lax.ppermute(scaled, "local", [(t[q], t[(q + step) % team]) for t in teams for q in range(team)])
        for step in range(team - 1, 0, -1)
    ]
    scaled_in = jnp.concatenate(around + [scaled], axis=0)
    rows_dy = rows_both[:, wide:]
    turned = lax.dynamic_slice_in_dim(
        jnp.concatenate([rows_dy, rows_dy], axis=0), (place // PAIR + 1) % team * own_rows, row_total, 0
    )

    def outer(rows, grads, first):
        return lax.dot_general(
            rows[:, first : first + width], grads, (((0,), (0,)), ((), ())), preferred_element_type=jnp.float32
        )

    def both_halves(rows, grads):
        came_half = lax.ppermute(outer(rows, grads, width).astype(jnp.bfloat16), "local", partners)
        return (outer(rows, grads, 0) + came_half.astype(jnp.float32)).astype(jnp.bfloat16)

    grad_gu = both_halves(rows_both[:, :wide], grads_in[:, : 2 * hidden_units])
    grad_d = both_halves(turned, scaled_in)

    token_sums = jnp.einsum("srt,rsd->td", selector_bf, came_terms[..., :wide], preferred_element_type=jnp.float32)
    came_stat = came_terms[..., wide].astype(jnp.float32).T
    stat_token = jnp.sum(jnp.where(selector, came_stat[:, :, None], 0.0), axis=0)
    prob_sums = jnp.sum(jnp.where(member, stat_token.T[:, None, :], 0.0), axis=2)
    tail = jnp.concatenate([token_sums[:, width:], prob_sums], axis=1).astype(jnp.bfloat16)
    came_tail = lax.ppermute(tail, "local", partners).astype(jnp.float32)
    grad_tokens = (token_sums[:, :width] + came_tail[:, :width]).astype(jnp.bfloat16)
    grad_probs = prob_sums + came_tail[:, width:]
    return (
        grad_tokens,
        grad_probs,
        grad_gu[None, :, :hidden_units],
        grad_gu[None, :, hidden_units:],
        grad_d[None],
    )


def solution(mesh):
    placed = (
        P("rack", "local"),
        P("rack", "local"),
        P("rack", None),
        P("rack", None),
        P("rack", "local", None),
        P("rack", "local", None),
        P("rack", "local", None),
    )
    return jax.shard_map(
        local,
        mesh=mesh,
        in_specs=placed,
        out_specs=(
            P("rack", "local"),
            P("rack", None),
            P("rack", "local", None),
            P("rack", "local", None),
            P("rack", "local", None),
        ),
        check_vma=False,
    )
```

```python
import jax
import jax.numpy as jnp
from jax import lax
from jax.experimental import pallas as pl
from jax.experimental.pallas import tpu as pltpu
from jax.sharding import PartitionSpec as P

RACKS_TOKEN = 4
LANES = 128
PAIR = 2
SIDE = 4


def activate(gate_pre, up_pre, back_proj, weights):
    logistic = jax.nn.sigmoid(gate_pre)
    active = gate_pre * logistic
    slope = logistic * (1.0 + gate_pre * (1.0 - logistic))
    hidden = active * up_pre
    statistic = jnp.sum(hidden * back_proj, axis=1)
    grad_hidden = weights[:, None] * back_proj
    grad_gate = (grad_hidden * up_pre * slope).astype(jnp.bfloat16)
    grad_up = (grad_hidden * active).astype(jnp.bfloat16)
    scaled = (weights[:, None] * hidden).astype(jnp.bfloat16)
    return (grad_gate, grad_up, scaled, statistic)


def exchange(rows, axis, groups=None):
    return lax.all_to_all(rows, axis, split_axis=0, concat_axis=0, tiled=True, axis_index_groups=groups)


def project(rows, weights, gate_up):
    count, lanes = rows.shape
    depth, columns = weights.shape
    tile = 4 * LANES

    def kernel(rows_ref, weights_ref, out_ref):
        step = pl.program_id(0)
        first = jnp.where(step < gate_up // tile, 0, (lanes - depth) // LANES)
        window = rows_ref[:, pl.ds(pl.multiple_of(first * LANES, LANES), depth)]
        columns_now = weights_ref[:, pl.ds(pl.multiple_of(step * tile, LANES), tile)]
        out_ref[...] = jnp.dot(window, columns_now, preferred_element_type=jnp.float32).astype(out_ref.dtype)

    return pl.pallas_call(
        kernel,
        grid=(columns // tile,),
        in_specs=[pl.BlockSpec(memory_space=pltpu.VMEM), pl.BlockSpec(memory_space=pltpu.VMEM)],
        out_specs=pl.BlockSpec((count, tile), lambda n: (0, n)),
        out_shape=jax.ShapeDtypeStruct((count, columns), rows.dtype),
        compiler_params=pltpu.CompilerParams(vmem_limit_bytes=16 * 1024 * 1024),
        cost_estimate=pl.CostEstimate(
            flops=2 * count * depth * columns,
            bytes_accessed=2 * (count * lanes + depth * columns + count * columns),
            transcendentals=0,
        ),
    )(rows, weights)


def local(x_tokens, cotangent, route_probs, expert_ids, w_gate, w_up, w_down):
    tok_count, width = x_tokens.shape
    rack_count = lax.axis_size("rack")
    local_count = lax.axis_size("local")
    team = local_count // PAIR
    teams = [[i for i in range(local_count) if (i % SIDE + 1) // 2 % PAIR == c] for c in range(PAIR)]
    partners = [(i, i ^ 1) for i in range(local_count)]
    place = lax.axis_index("local")
    slots = 5 * RACKS_TOKEN * tok_count // (4 * rack_count) // PAIR
    row_total = rack_count * slots
    own_rows = row_total // team
    hidden_units = w_gate.shape[2]
    wide = PAIR * width

    x_cols, dy_cols = x_tokens.T, cotangent.T
    own = lax.optimization_barrier(jnp.concatenate([x_cols, dy_cols], axis=0))
    other = lax.ppermute(own, "local", partners)
    tokens = lax.optimization_barrier(
        jnp.concatenate([own[:width], other[:width], own[width:], other[width:]], axis=0)
    )

    rack_ids = jnp.arange(rack_count, dtype=jnp.int32)
    member = expert_ids[:, :, None] == rack_ids[None, None, :]
    in_use = jnp.any(member, axis=1)
    slot_rank = jnp.cumsum(in_use.astype(jnp.int32), axis=0) - 1
    slot_ids = jnp.arange(slots, dtype=jnp.int32) + (place % SIDE + 1) // 2 % PAIR * slots
    selector = in_use.T[None, :, :] & (slot_rank.T[None, :, :] == slot_ids[:, None, None])
    selector_bf = selector.astype(jnp.bfloat16)
    prob_rack = jnp.sum(jnp.where(member, route_probs.astype(jnp.float32)[:, :, None], 0.0), axis=1)
    send_prob = jnp.sum(jnp.where(selector, prob_rack.T[None, :, :], 0.0), axis=2).astype(jnp.bfloat16)

    chunks = PAIR * wide // LANES
    picked = [
        jnp.einsum(
            "srt,dt->srd", selector_bf, tokens[k * LANES : (k + 1) * LANES], preferred_element_type=jnp.float32
        ).astype(jnp.bfloat16)
        for k in range(chunks)
    ]
    picked.append(jnp.pad(send_prob.T, ((0, 0), (0, LANES - slots)))[None])
    message = jnp.concatenate(picked, axis=0)
    message_rows = message.shape[0]
    message = message.transpose(1, 0, 2).reshape(rack_count, message_rows // 2, 2, LANES)
    message, w_gate, w_up, w_down = lax.optimization_barrier((message, w_gate, w_up, w_down))
    came = exchange(message, "rack")
    came = came.reshape(rack_count, message_rows, LANES).transpose(1, 0, 2)
    rows_both = jnp.concatenate(
        [came[k * slots : (k + 1) * slots].reshape(row_total, LANES) for k in range(chunks)], axis=1
    )
    rows_prob = came[message_rows - 1, :, :slots].T.reshape(row_total).astype(jnp.float32)

    own_weights = jnp.concatenate([w_gate[0], w_up[0], w_down[0]], axis=1)
    other_weights = lax.ppermute(own_weights, "local", partners)
    weights = jnp.concatenate([own_weights, other_weights], axis=0)
    weight_gu, weight_down = weights[:, : 2 * hidden_units], weights[:, 2 * hidden_units :]
    depth = (wide + LANES - 1) // LANES * LANES
    filled = lax.optimization_barrier(
        jnp.concatenate(
            [
                jnp.pad(weight_gu, ((0, depth - wide), (0, 0))),
                jnp.pad(weight_down, ((depth - wide, 0), (0, 0))),
            ],
            axis=1,
        )
    )
    own_prob = lax.dynamic_slice_in_dim(rows_prob, place // PAIR * own_rows, own_rows, 0)
    own_prob, rows_both = lax.optimization_barrier((own_prob, rows_both))
    partial = project(rows_both, filled, 2 * hidden_units)
    parts = exchange(partial.reshape(team, own_rows, 3 * hidden_units), "local", teams)
    sums = jnp.sum(parts.astype(jnp.float32), axis=0)

    grad_gate, grad_up, scaled, statistic = activate(
        sums[:, :hidden_units], sums[:, hidden_units : 2 * hidden_units], sums[:, 2 * hidden_units :], own_prob
    )
    stat_lanes = jnp.broadcast_to(statistic.astype(jnp.bfloat16)[:, None], (own_rows, LANES))
    packed = jnp.concatenate([grad_gate, grad_up, scaled, stat_lanes], axis=1)
    grads_in = exchange(jnp.broadcast_to(packed[None], (team,) + packed.shape), "local", teams)
    grads_in = grads_in.reshape(row_total, 3 * hidden_units + LANES)
    stats_in = grads_in[:, 3 * hidden_units : 3 * hidden_units + 1]

    term = lax.dot_general(
        grads_in[:, : 2 * hidden_units],
        filled[:wide, : 2 * hidden_units],
        (((1,), (1,)), ((), ())),
        preferred_element_type=jnp.float32,
    ).astype(jnp.bfloat16)
    back = jnp.concatenate([term, jnp.broadcast_to(stats_in, (row_total, depth - wide))], axis=1)
    back = back.reshape(slots, rack_count, depth // LANES, LANES).transpose(1, 0, 2, 3)
    back, rows_both, grads_in = lax.optimization_barrier((back, rows_both, grads_in))
    came_terms = exchange(back, "rack").reshape(rack_count, slots, depth)

    rows_x, rows_dy = rows_both[:, :wide], rows_both[:, wide:]
    gate_up_in = grads_in[:, : 2 * hidden_units]
    scaled_in = grads_in[:, 2 * hidden_units : 3 * hidden_units]

    def outer(rows, grads, first):
        return lax.dot_general(
            rows[:, first : first + width], grads, (((0,), (0,)), ((), ())), preferred_element_type=jnp.float32
        )

    def both(first):
        return jnp.concatenate([outer(rows_x, gate_up_in, first), outer(rows_dy, scaled_in, first)], axis=1)

    came_grads = lax.ppermute(both(width).astype(jnp.bfloat16), "local", partners)
    grads = (both(0) + came_grads.astype(jnp.float32)).astype(jnp.bfloat16)

    token_sums = jnp.einsum("srt,rsd->td", selector_bf, came_terms[..., :wide], preferred_element_type=jnp.float32)
    came_stat = came_terms[..., wide].astype(jnp.float32).T
    stat_token = jnp.sum(jnp.where(selector, came_stat[:, :, None], 0.0), axis=0)
    prob_sums = jnp.sum(jnp.where(member, stat_token.T[:, None, :], 0.0), axis=2)
    tail = jnp.concatenate([token_sums[:, width:], prob_sums], axis=1).astype(jnp.bfloat16)
    came_tail = lax.ppermute(tail, "local", partners).astype(jnp.float32)
    grad_tokens = (token_sums[:, :width] + came_tail[:, :width]).astype(jnp.bfloat16)
    grad_probs = prob_sums + came_tail[:, width:]
    return (
        grad_tokens,
        grad_probs,
        grads[None, :, :hidden_units],
        grads[None, :, hidden_units : 2 * hidden_units],
        grads[None, :, 2 * hidden_units :],
    )


def solution(mesh):
    placed = (
        P("rack", "local"),
        P("rack", "local"),
        P("rack", None),
        P("rack", None),
        P("rack", "local", None),
        P("rack", "local", None),
        P("rack", "local", None),
    )
    return jax.shard_map(
        local,
        mesh=mesh,
        in_specs=placed,
        out_specs=(
            P("rack", "local"),
            P("rack", None),
            P("rack", "local", None),
            P("rack", "local", None),
            P("rack", "local", None),
        ),
        check_vma=False,
    )
```

```python
import jax
import jax.numpy as jnp
from jax import lax
from jax.experimental import pallas as pl
from jax.experimental.pallas import tpu as pltpu
from jax.sharding import PartitionSpec as P

RACKS_TOKEN = 4
LANES = 128
PAIR = 2
SIDE = 4


def activate(gate_pre, up_pre, back_proj, weights):
    logistic = jax.nn.sigmoid(gate_pre)
    active = gate_pre * logistic
    slope = logistic * (1.0 + gate_pre * (1.0 - logistic))
    hidden = active * up_pre
    statistic = jnp.sum(hidden * back_proj, axis=1)
    grad_hidden = weights[:, None] * back_proj
    grad_gate = (grad_hidden * up_pre * slope).astype(jnp.bfloat16)
    grad_up = (grad_hidden * active).astype(jnp.bfloat16)
    scaled = (weights[:, None] * hidden).astype(jnp.bfloat16)
    return (grad_gate, grad_up, scaled, statistic)


def exchange(rows, axis, groups=None):
    return lax.all_to_all(rows, axis, split_axis=0, concat_axis=0, tiled=True, axis_index_groups=groups)


def unpack(came, slots):
    count, racks, _ = came.shape
    chunks = count // slots
    total = slots * racks

    def kernel(came_ref, rows_ref):
        for k in range(chunks):
            rows_ref[:, k * LANES : (k + 1) * LANES] = came_ref[k * slots : (k + 1) * slots].reshape(total, LANES)

    return pl.pallas_call(
        kernel,
        out_shape=jax.ShapeDtypeStruct((total, chunks * LANES), came.dtype),
        compiler_params=pltpu.CompilerParams(vmem_limit_bytes=16 * 1024 * 1024),
    )(came)


def project(rows, weights, gate_up):
    count, lanes = rows.shape
    depth, columns = weights.shape
    tile = 4 * LANES

    def kernel(rows_ref, weights_ref, out_ref):
        step = pl.program_id(0)
        first = jnp.where(step < gate_up // tile, 0, (lanes - depth) // LANES)
        window = rows_ref[:, pl.ds(pl.multiple_of(first * LANES, LANES), depth)]
        columns_now = weights_ref[:, pl.ds(pl.multiple_of(step * tile, LANES), tile)]
        out_ref[...] = jnp.dot(window, columns_now, preferred_element_type=jnp.float32).astype(out_ref.dtype)

    return pl.pallas_call(
        kernel,
        grid=(columns // tile,),
        in_specs=[pl.BlockSpec(memory_space=pltpu.VMEM), pl.BlockSpec(memory_space=pltpu.VMEM)],
        out_specs=pl.BlockSpec((count, tile), lambda n: (0, n)),
        out_shape=jax.ShapeDtypeStruct((count, columns), rows.dtype),
        compiler_params=pltpu.CompilerParams(vmem_limit_bytes=16 * 1024 * 1024),
        cost_estimate=pl.CostEstimate(
            flops=2 * count * depth * columns,
            bytes_accessed=2 * (count * lanes + depth * columns + count * columns),
            transcendentals=0,
        ),
    )(rows, weights)


def finish(own_sums, own_probs, came):
    width = came.shape[0] - own_probs.shape[0]

    def kernel(sums_ref, probs_ref, came_ref, tokens_ref, out_probs_ref):
        tokens_ref[...] = (sums_ref[...] + came_ref[:width].astype(jnp.float32)).astype(tokens_ref.dtype)
        out_probs_ref[...] = probs_ref[...] + came_ref[width:].astype(jnp.float32)

    return pl.pallas_call(
        kernel,
        out_shape=[
            jax.ShapeDtypeStruct((width, came.shape[1]), came.dtype),
            jax.ShapeDtypeStruct(own_probs.shape, jnp.float32),
        ],
        compiler_params=pltpu.CompilerParams(vmem_limit_bytes=16 * 1024 * 1024),
    )(own_sums, own_probs, came)


def local(x_tokens, cotangent, route_probs, expert_ids, w_gate, w_up, w_down):
    tok_count, width = x_tokens.shape
    rack_count = lax.axis_size("rack")
    local_count = lax.axis_size("local")
    team = local_count // PAIR
    teams = [[i for i in range(local_count) if (i % SIDE + 1) // 2 % PAIR == c] for c in range(PAIR)]
    partners = [(i, i ^ 1) for i in range(local_count)]
    place = lax.axis_index("local")
    slots = 5 * RACKS_TOKEN * tok_count // (4 * rack_count) // PAIR
    row_total = rack_count * slots
    own_rows = row_total // team
    hidden_units = w_gate.shape[2]
    wide = PAIR * width

    x_cols, dy_cols = x_tokens.T, cotangent.T
    own = lax.optimization_barrier(jnp.concatenate([x_cols, dy_cols], axis=0))
    other = lax.ppermute(own, "local", partners)
    tokens = lax.optimization_barrier(
        jnp.concatenate([own[:width], other[:width], own[width:], other[width:]], axis=0)
    )

    rack_ids = jnp.arange(rack_count, dtype=jnp.int32)
    member = expert_ids[:, :, None] == rack_ids[None, None, :]
    in_use = jnp.any(member, axis=1)
    slot_rank = jnp.cumsum(in_use.astype(jnp.int32), axis=0) - 1
    slot_ids = jnp.arange(slots, dtype=jnp.int32) + (place % SIDE + 1) // 2 % PAIR * slots
    selector = in_use.T[None, :, :] & (slot_rank.T[None, :, :] == slot_ids[:, None, None])
    selector_bf = selector.astype(jnp.bfloat16)
    prob_rack = jnp.sum(jnp.where(member, route_probs.astype(jnp.float32)[:, :, None], 0.0), axis=1)
    send_prob = jnp.sum(jnp.where(selector, prob_rack.T[None, :, :], 0.0), axis=2).astype(jnp.bfloat16)

    chunks = PAIR * wide // LANES
    picked = [
        jnp.einsum(
            "srt,dt->srd", selector_bf, tokens[k * LANES : (k + 1) * LANES], preferred_element_type=jnp.float32
        ).astype(jnp.bfloat16)
        for k in range(chunks)
    ]
    picked.append(jnp.pad(send_prob.T, ((0, 0), (0, LANES - slots)))[None])
    message = jnp.concatenate(picked, axis=0)
    message_rows = message.shape[0]
    message = message.transpose(1, 0, 2).reshape(rack_count, message_rows // 2, 2, LANES)
    own_ids = place // PAIR * own_rows + jnp.arange(own_rows, dtype=jnp.int32)
    row_ids = jnp.arange(rack_count, dtype=jnp.int32)[:, None] + rack_count * jnp.arange(slots, dtype=jnp.int32)
    own_mask = (own_ids[:, None, None] == row_ids).astype(jnp.float32)
    message, w_gate, w_up, w_down, own_mask = lax.optimization_barrier((message, w_gate, w_up, w_down, own_mask))
    came = exchange(message, "rack")
    came = came.reshape(rack_count, message_rows, LANES).transpose(1, 0, 2)

    own_weights = jnp.concatenate([w_gate[0], w_up[0], w_down[0]], axis=1)
    other_weights = lax.ppermute(own_weights, "local", partners)
    weights = jnp.concatenate([own_weights, other_weights], axis=0)
    weight_gu, weight_down = weights[:, : 2 * hidden_units], weights[:, 2 * hidden_units :]
    depth = (wide + LANES - 1) // LANES * LANES
    filled = lax.optimization_barrier(
        jnp.concatenate(
            [
                jnp.pad(weight_gu, ((0, depth - wide), (0, 0))),
                jnp.pad(weight_down, ((depth - wide, 0), (0, 0))),
            ],
            axis=1,
        )
    )
    came_prob = came[message_rows - 1, :, :slots].astype(jnp.float32)
    came_prob, came = lax.optimization_barrier((came_prob, came))
    rows_both = unpack(came, slots)
    partial = project(rows_both, filled, 2 * hidden_units)
    parts = exchange(partial.reshape(team, own_rows, 3 * hidden_units), "local", teams)
    parts, came_prob = lax.optimization_barrier((parts, came_prob))
    own_prob = jnp.sum(own_mask * came_prob, axis=(1, 2))
    sums = jnp.sum(parts.astype(jnp.float32), axis=0)

    grad_gate, grad_up, scaled, statistic = activate(
        sums[:, :hidden_units], sums[:, hidden_units : 2 * hidden_units], sums[:, 2 * hidden_units :], own_prob
    )
    stat_lanes = jnp.broadcast_to(statistic.astype(jnp.bfloat16)[:, None], (own_rows, LANES))
    packed = jnp.concatenate([grad_gate, grad_up, stat_lanes], axis=1)
    grads_in = exchange(jnp.broadcast_to(packed[None], (team,) + packed.shape), "local", teams)
    grads_in = grads_in.reshape(row_total, 2 * hidden_units + LANES)
    stats_in = grads_in[:, 2 * hidden_units : 2 * hidden_units + 1]

    term = lax.dot_general(
        grads_in[:, : 2 * hidden_units],
        filled[:wide, : 2 * hidden_units],
        (((1,), (1,)), ((), ())),
        preferred_element_type=jnp.float32,
    ).astype(jnp.bfloat16)
    back = jnp.concatenate([term, jnp.broadcast_to(stats_in, (row_total, depth - wide))], axis=1)
    back = back.reshape(slots, rack_count, depth // LANES, LANES).transpose(1, 0, 2, 3)
    back, rows_both, grads_in, scaled = lax.optimization_barrier((back, rows_both, grads_in, scaled))
    came_terms = exchange(back, "rack").reshape(rack_count, slots, depth)

    def outer(rows, grads, first):
        return lax.dot_general(
            rows[:, first : first + width], grads, (((0,), (0,)), ((), ())), preferred_element_type=jnp.float32
        )

    rows_x, rows_dy = rows_both[:, :wide], rows_both[:, wide:]
    gate_up_in = grads_in[:, : 2 * hidden_units]
    send_gu = outer(rows_x, gate_up_in, width).astype(jnp.bfloat16)
    piece = 2 * SIDE * PAIR
    first_gu = lax.ppermute(send_gu[:piece], "local", partners)
    other_gu = lax.ppermute(send_gu[piece:], "local", partners)
    first_gu, scaled = lax.optimization_barrier((first_gu, scaled))
    came_gu = jnp.concatenate([first_gu, other_gu], axis=0).astype(jnp.float32)
    grad_gu = (outer(rows_x, gate_up_in, 0) + came_gu).astype(jnp.bfloat16)

    around = [
        lax.ppermute(scaled, "local", [(t[q], t[(q + step) % team]) for t in teams for q in range(team)])
        for step in range(team - 1, 0, -1)
    ]
    scaled_in = jnp.concatenate(around + [scaled], axis=0)
    turned = lax.dynamic_slice_in_dim(
        jnp.concatenate([rows_dy, rows_dy], axis=0), (place // PAIR + 1) % team * own_rows, row_total, 0
    )
    came_d = lax.ppermute(outer(turned, scaled_in, width).astype(jnp.bfloat16), "local", partners)
    grad_d = (outer(turned, scaled_in, 0) + came_d.astype(jnp.float32)).astype(jnp.bfloat16)

    token_sums = jnp.einsum("srt,rsd->dt", selector_bf, came_terms[..., :wide], preferred_element_type=jnp.float32)
    came_stat = came_terms[..., wide].astype(jnp.float32).T
    stat_token = jnp.sum(jnp.where(selector, came_stat[:, :, None], 0.0), axis=0)
    prob_sums = jnp.sum(jnp.where(member, stat_token.T[:, None, :], 0.0), axis=2).T
    tail = jnp.concatenate([token_sums[width:], prob_sums], axis=0).astype(jnp.bfloat16)
    came_tail = lax.ppermute(tail, "local", partners)
    token_cols, prob_cols = finish(token_sums[:width], prob_sums, came_tail)
    return (
        token_cols.T,
        prob_cols.T,
        grad_gu[None, :, :hidden_units],
        grad_gu[None, :, hidden_units:],
        grad_d[None],
    )


def solution(mesh):
    placed = (
        P("rack", "local"),
        P("rack", "local"),
        P("rack", None),
        P("rack", None),
        P("rack", "local", None),
        P("rack", "local", None),
        P("rack", "local", None),
    )
    return jax.shard_map(
        local,
        mesh=mesh,
        in_specs=placed,
        out_specs=(
            P("rack", "local"),
            P("rack", None),
            P("rack", "local", None),
            P("rack", "local", None),
            P("rack", "local", None),
        ),
        check_vma=False,
    )
```

```python
import jax
import jax.numpy as jnp
from jax import lax
from jax.experimental import pallas as pl
from jax.experimental.pallas import tpu as pltpu
from jax.sharding import PartitionSpec as P

RACKS_TOKEN = 4
LANES = 128
PAIR = 2
SIDE = 4


def activate(gate_pre, up_pre, back_proj, weights):
    logistic = jax.nn.sigmoid(gate_pre)
    active = gate_pre * logistic
    slope = logistic * (1.0 + gate_pre * (1.0 - logistic))
    hidden = active * up_pre
    statistic = jnp.sum(hidden * back_proj, axis=1)
    grad_hidden = weights[:, None] * back_proj
    grad_gate = (grad_hidden * up_pre * slope).astype(jnp.bfloat16)
    grad_up = (grad_hidden * active).astype(jnp.bfloat16)
    scaled = (weights[:, None] * hidden).astype(jnp.bfloat16)
    return (grad_gate, grad_up, scaled, statistic)


def exchange(rows, axis, groups=None):
    return lax.all_to_all(rows, axis, split_axis=0, concat_axis=0, tiled=True, axis_index_groups=groups)


def unpack(came, slots):
    count, racks, _ = came.shape
    chunks = count // slots
    total = slots * racks

    def kernel(came_ref, rows_ref):
        for k in range(chunks):
            rows_ref[:, k * LANES : (k + 1) * LANES] = came_ref[k * slots : (k + 1) * slots].reshape(total, LANES)

    return pl.pallas_call(
        kernel,
        out_shape=jax.ShapeDtypeStruct((total, chunks * LANES), came.dtype),
        compiler_params=pltpu.CompilerParams(vmem_limit_bytes=16 * 1024 * 1024),
    )(came)


def project(rows, weights, gate_up):
    count, lanes = rows.shape
    depth, columns = weights.shape
    tile = 4 * LANES

    def kernel(rows_ref, weights_ref, out_ref):
        step = pl.program_id(0)
        first = jnp.where(step < gate_up // tile, 0, (lanes - depth) // LANES)
        window = rows_ref[:, pl.ds(pl.multiple_of(first * LANES, LANES), depth)]
        columns_now = weights_ref[:, pl.ds(pl.multiple_of(step * tile, LANES), tile)]
        out_ref[...] = jnp.dot(window, columns_now, preferred_element_type=jnp.float32).astype(out_ref.dtype)

    return pl.pallas_call(
        kernel,
        grid=(columns // tile,),
        in_specs=[pl.BlockSpec(memory_space=pltpu.VMEM), pl.BlockSpec(memory_space=pltpu.VMEM)],
        out_specs=pl.BlockSpec((count, tile), lambda n: (0, n)),
        out_shape=jax.ShapeDtypeStruct((count, columns), rows.dtype),
        compiler_params=pltpu.CompilerParams(vmem_limit_bytes=16 * 1024 * 1024),
        cost_estimate=pl.CostEstimate(
            flops=2 * count * depth * columns,
            bytes_accessed=2 * (count * lanes + depth * columns + count * columns),
            transcendentals=0,
        ),
    )(rows, weights)


def finish(own_sums, own_probs, came):
    width = came.shape[0] - own_probs.shape[0]

    def kernel(sums_ref, probs_ref, came_ref, tokens_ref, out_probs_ref):
        tokens_ref[...] = (sums_ref[...] + came_ref[:width].astype(jnp.float32)).astype(tokens_ref.dtype)
        out_probs_ref[...] = probs_ref[...] + came_ref[width:].astype(jnp.float32)

    return pl.pallas_call(
        kernel,
        out_shape=[
            jax.ShapeDtypeStruct((width, came.shape[1]), came.dtype),
            jax.ShapeDtypeStruct(own_probs.shape, jnp.float32),
        ],
        compiler_params=pltpu.CompilerParams(vmem_limit_bytes=16 * 1024 * 1024),
    )(own_sums, own_probs, came)


def local(x_tokens, cotangent, route_probs, expert_ids, w_gate, w_up, w_down):
    tok_count, width = x_tokens.shape
    rack_count = lax.axis_size("rack")
    local_count = lax.axis_size("local")
    team = local_count // PAIR
    teams = [[i for i in range(local_count) if (i % SIDE + 1) // 2 % PAIR == c] for c in range(PAIR)]
    partners = [(i, i ^ 1) for i in range(local_count)]
    place = lax.axis_index("local")
    slots = 5 * RACKS_TOKEN * tok_count // (4 * rack_count) // PAIR
    row_total = rack_count * slots
    own_rows = row_total // team
    hidden_units = w_gate.shape[2]
    wide = PAIR * width

    x_cols, dy_cols = x_tokens.T, cotangent.T
    own = lax.optimization_barrier(jnp.concatenate([x_cols, dy_cols], axis=0))
    other = lax.ppermute(own, "local", partners)
    tokens = lax.optimization_barrier(
        jnp.concatenate([own[:width], other[:width], own[width:], other[width:]], axis=0)
    )

    rack_ids = jnp.arange(rack_count, dtype=jnp.int32)
    member = expert_ids[:, :, None] == rack_ids[None, None, :]
    in_use = jnp.any(member, axis=1)
    slot_rank = jnp.cumsum(in_use.astype(jnp.int32), axis=0) - 1
    slot_ids = jnp.arange(slots, dtype=jnp.int32) + (place % SIDE + 1) // 2 % PAIR * slots
    selector = in_use.T[None, :, :] & (slot_rank.T[None, :, :] == slot_ids[:, None, None])
    selector_bf = selector.astype(jnp.bfloat16)
    prob_rack = jnp.sum(jnp.where(member, route_probs.astype(jnp.float32)[:, :, None], 0.0), axis=1)
    send_prob = jnp.sum(jnp.where(selector, prob_rack.T[None, :, :], 0.0), axis=2).astype(jnp.bfloat16)

    chunks = PAIR * wide // LANES
    picked = [
        jnp.einsum(
            "srt,dt->srd", selector_bf, tokens[k * LANES : (k + 1) * LANES], preferred_element_type=jnp.float32
        ).astype(jnp.bfloat16)
        for k in range(chunks)
    ]
    picked.append(jnp.pad(send_prob.T, ((0, 0), (0, LANES - slots)))[None])
    message = jnp.concatenate(picked, axis=0)
    message_rows = message.shape[0]
    message = message.transpose(1, 0, 2).reshape(rack_count, message_rows // 2, 2, LANES)
    own_ids = place // PAIR * own_rows + jnp.arange(own_rows, dtype=jnp.int32)
    row_ids = jnp.arange(rack_count, dtype=jnp.int32)[:, None] + rack_count * jnp.arange(slots, dtype=jnp.int32)
    own_mask = (own_ids[:, None, None] == row_ids).astype(jnp.float32)
    message, w_gate, w_up, w_down, own_mask = lax.optimization_barrier((message, w_gate, w_up, w_down, own_mask))
    came = exchange(message, "rack")
    came = came.reshape(rack_count, message_rows, LANES).transpose(1, 0, 2)

    own_weights = jnp.concatenate([w_gate[0], w_up[0], w_down[0]], axis=1)
    other_weights = lax.ppermute(own_weights, "local", partners)
    weights = jnp.concatenate([own_weights, other_weights], axis=0)
    weight_gu, weight_down = weights[:, : 2 * hidden_units], weights[:, 2 * hidden_units :]
    depth = (wide + LANES - 1) // LANES * LANES
    filled = lax.optimization_barrier(
        jnp.concatenate(
            [
                jnp.pad(weight_gu, ((0, depth - wide), (0, 0))),
                jnp.pad(weight_down, ((depth - wide, 0), (0, 0))),
            ],
            axis=1,
        )
    )
    came_prob = came[message_rows - 1, :, :slots].astype(jnp.float32)
    came_prob, came = lax.optimization_barrier((came_prob, came))
    rows_both = unpack(came, slots)
    partial = project(rows_both, filled, 2 * hidden_units)
    parts = exchange(partial.reshape(team, own_rows, 3 * hidden_units), "local", teams)
    parts, came_prob = lax.optimization_barrier((parts, came_prob))
    own_prob = jnp.sum(own_mask * came_prob, axis=(1, 2))
    sums = jnp.sum(parts.astype(jnp.float32), axis=0)

    grad_gate, grad_up, scaled, statistic = activate(
        sums[:, :hidden_units], sums[:, hidden_units : 2 * hidden_units], sums[:, 2 * hidden_units :], own_prob
    )
    stat_lanes = jnp.broadcast_to(statistic.astype(jnp.bfloat16)[:, None], (own_rows, LANES))
    packed = jnp.concatenate([grad_gate, grad_up, stat_lanes], axis=1)
    grads_in = exchange(jnp.broadcast_to(packed[None], (team,) + packed.shape), "local", teams)
    grads_in = grads_in.reshape(row_total, 2 * hidden_units + LANES)
    stats_in = grads_in[:, 2 * hidden_units : 2 * hidden_units + 1]

    term = lax.dot_general(
        grads_in[:, : 2 * hidden_units],
        filled[:wide, : 2 * hidden_units],
        (((1,), (1,)), ((), ())),
        preferred_element_type=jnp.float32,
    ).astype(jnp.bfloat16)
    back = jnp.concatenate([term, jnp.broadcast_to(stats_in, (row_total, depth - wide))], axis=1)
    back = back.reshape(slots, rack_count, depth // LANES, LANES).transpose(1, 0, 2, 3)
    back, rows_both, grads_in, scaled = lax.optimization_barrier((back, rows_both, grads_in, scaled))
    came_terms = exchange(back, "rack").reshape(rack_count, slots, depth)

    def outer(rows, grads, first):
        return lax.dot_general(
            rows[:, first : first + width], grads, (((0,), (0,)), ((), ())), preferred_element_type=jnp.float32
        )

    rows_x, rows_dy = rows_both[:, :wide], rows_both[:, wide:]
    gate_up_in = grads_in[:, : 2 * hidden_units]
    send_gu = outer(rows_x, gate_up_in, width).astype(jnp.bfloat16)
    piece = 2 * SIDE * PAIR
    first_gu = lax.ppermute(send_gu[:piece], "local", partners)
    other_gu = lax.ppermute(send_gu[piece:], "local", partners)
    first_gu, scaled = lax.optimization_barrier((first_gu, scaled))
    came_gu = jnp.concatenate([first_gu, other_gu], axis=0).astype(jnp.float32)
    grad_gu = (outer(rows_x, gate_up_in, 0) + came_gu).astype(jnp.bfloat16)

    row, column = place // SIDE, place % SIDE
    across = [(i, i // SIDE * SIDE + SIDE - 1 - i % SIDE) for i in range(local_count)]
    two = jnp.concatenate([scaled, lax.ppermute(scaled, "local", across)], axis=0)
    sides = local_count // SIDE
    around = [
        lax.ppermute(two, "local", [(i, (i + SIDE * step) % local_count) for i in range(local_count)])
        for step in range(sides - 1, 0, -1)
    ]
    scaled_in = jnp.concatenate(around + [two], axis=0)
    rows_split = rows_dy.reshape(sides, PAIR, own_rows, wide)
    rows_split = jnp.where(column < PAIR, rows_split, rows_split[:, ::-1])
    turned = lax.dynamic_slice_in_dim(
        jnp.concatenate([rows_split, rows_split], axis=0), (row + 1) % sides, sides, 0
    ).reshape(row_total, wide)
    came_d = lax.ppermute(outer(turned, scaled_in, width).astype(jnp.bfloat16), "local", partners)
    grad_d = (outer(turned, scaled_in, 0) + came_d.astype(jnp.float32)).astype(jnp.bfloat16)

    token_sums = jnp.einsum("srt,rsd->dt", selector_bf, came_terms[..., :wide], preferred_element_type=jnp.float32)
    came_stat = came_terms[..., wide].astype(jnp.float32).T
    stat_token = jnp.sum(jnp.where(selector, came_stat[:, :, None], 0.0), axis=0)
    prob_sums = jnp.sum(jnp.where(member, stat_token.T[:, None, :], 0.0), axis=2).T
    tail = jnp.concatenate([token_sums[width:], prob_sums], axis=0).astype(jnp.bfloat16)
    came_tail = lax.ppermute(tail, "local", partners)
    token_cols, prob_cols = finish(token_sums[:width], prob_sums, came_tail)
    return (
        token_cols.T,
        prob_cols.T,
        grad_gu[None, :, :hidden_units],
        grad_gu[None, :, hidden_units:],
        grad_d[None],
    )


def solution(mesh):
    placed = (
        P("rack", "local"),
        P("rack", "local"),
        P("rack", None),
        P("rack", None),
        P("rack", "local", None),
        P("rack", "local", None),
        P("rack", "local", None),
    )
    return jax.shard_map(
        local,
        mesh=mesh,
        in_specs=placed,
        out_specs=(
            P("rack", "local"),
            P("rack", None),
            P("rack", "local", None),
            P("rack", "local", None),
            P("rack", "local", None),
        ),
        check_vma=False,
    )
```

```python
import jax
import jax.numpy as jnp
from jax import lax
from jax.experimental import pallas as pl
from jax.experimental.pallas import tpu as pltpu
from jax.sharding import PartitionSpec as P

RACKS_TOKEN = 4
LANES = 128
PAIR = 2
SIDE = 4


def activate(gate_pre, up_pre, back_proj, weights):
    logistic = jax.nn.sigmoid(gate_pre)
    active = gate_pre * logistic
    slope = logistic * (1.0 + gate_pre * (1.0 - logistic))
    hidden = active * up_pre
    statistic = jnp.sum(hidden * back_proj, axis=1)
    grad_hidden = weights[:, None] * back_proj
    grad_gate = (grad_hidden * up_pre * slope).astype(jnp.bfloat16)
    grad_up = (grad_hidden * active).astype(jnp.bfloat16)
    scaled = (weights[:, None] * hidden).astype(jnp.bfloat16)
    return (grad_gate, grad_up, scaled, statistic)


def exchange(rows, axis, groups=None):
    return lax.all_to_all(rows, axis, split_axis=0, concat_axis=0, tiled=True, axis_index_groups=groups)


def unpack(came, slots):
    count, racks, _ = came.shape
    chunks = count // slots
    total = slots * racks

    def kernel(came_ref, rows_ref):
        for k in range(chunks):
            rows_ref[:, k * LANES : (k + 1) * LANES] = came_ref[k * slots : (k + 1) * slots].reshape(total, LANES)

    return pl.pallas_call(
        kernel,
        out_shape=jax.ShapeDtypeStruct((total, chunks * LANES), came.dtype),
        compiler_params=pltpu.CompilerParams(vmem_limit_bytes=16 * 1024 * 1024),
    )(came)


def project(rows, weights, gate_up):
    count, lanes = rows.shape
    depth, columns = weights.shape
    tile = 4 * LANES

    def kernel(rows_ref, weights_ref, out_ref):
        step = pl.program_id(0)
        first = jnp.where(step < gate_up // tile, 0, (lanes - depth) // LANES)
        window = rows_ref[:, pl.ds(pl.multiple_of(first * LANES, LANES), depth)]
        columns_now = weights_ref[:, pl.ds(pl.multiple_of(step * tile, LANES), tile)]
        out_ref[...] = jnp.dot(window, columns_now, preferred_element_type=jnp.float32).astype(out_ref.dtype)

    return pl.pallas_call(
        kernel,
        grid=(columns // tile,),
        in_specs=[pl.BlockSpec(memory_space=pltpu.VMEM), pl.BlockSpec(memory_space=pltpu.VMEM)],
        out_specs=pl.BlockSpec((count, tile), lambda n: (0, n)),
        out_shape=jax.ShapeDtypeStruct((count, columns), rows.dtype),
        compiler_params=pltpu.CompilerParams(vmem_limit_bytes=16 * 1024 * 1024),
        cost_estimate=pl.CostEstimate(
            flops=2 * count * depth * columns,
            bytes_accessed=2 * (count * lanes + depth * columns + count * columns),
            transcendentals=0,
        ),
    )(rows, weights)


def finish(own_sums, own_probs, came):
    width = came.shape[0] - own_probs.shape[0]

    def kernel(sums_ref, probs_ref, came_ref, tokens_ref, out_probs_ref):
        tokens_ref[...] = (sums_ref[...] + came_ref[:width].astype(jnp.float32)).astype(tokens_ref.dtype)
        out_probs_ref[...] = probs_ref[...] + came_ref[width:].astype(jnp.float32)

    return pl.pallas_call(
        kernel,
        out_shape=[
            jax.ShapeDtypeStruct((width, came.shape[1]), came.dtype),
            jax.ShapeDtypeStruct(own_probs.shape, jnp.float32),
        ],
        compiler_params=pltpu.CompilerParams(vmem_limit_bytes=16 * 1024 * 1024),
    )(own_sums, own_probs, came)


def local(x_tokens, cotangent, route_probs, expert_ids, w_gate, w_up, w_down):
    tok_count, width = x_tokens.shape
    rack_count = lax.axis_size("rack")
    local_count = lax.axis_size("local")
    team = local_count // PAIR
    teams = [[i for i in range(local_count) if (i % SIDE + 1) // 2 % PAIR == c] for c in range(PAIR)]
    partners = [(i, i ^ 1) for i in range(local_count)]
    place = lax.axis_index("local")
    slots = 5 * RACKS_TOKEN * tok_count // (4 * rack_count) // PAIR
    row_total = rack_count * slots
    own_rows = row_total // team
    hidden_units = w_gate.shape[2]
    wide = PAIR * width

    x_cols, dy_cols = x_tokens.T, cotangent.T
    own = lax.optimization_barrier(jnp.concatenate([x_cols, dy_cols], axis=0))
    other = lax.ppermute(own, "local", partners)
    tokens = lax.optimization_barrier(
        jnp.concatenate([own[:width], other[:width], own[width:], other[width:]], axis=0)
    )

    rack_ids = jnp.arange(rack_count, dtype=jnp.int32)
    member = expert_ids[:, :, None] == rack_ids[None, None, :]
    in_use = jnp.any(member, axis=1)
    slot_rank = jnp.cumsum(in_use.astype(jnp.int32), axis=0) - 1
    slot_ids = jnp.arange(slots, dtype=jnp.int32) + (place % SIDE + 1) // 2 % PAIR * slots
    selector = in_use.T[None, :, :] & (slot_rank.T[None, :, :] == slot_ids[:, None, None])
    selector_bf = selector.astype(jnp.bfloat16)
    prob_rack = jnp.sum(jnp.where(member, route_probs.astype(jnp.float32)[:, :, None], 0.0), axis=1)
    send_prob = jnp.sum(jnp.where(selector, prob_rack.T[None, :, :], 0.0), axis=2).astype(jnp.bfloat16)

    chunks = PAIR * wide // LANES
    picked = [
        jnp.einsum(
            "srt,dt->srd", selector_bf, tokens[k * LANES : (k + 1) * LANES], preferred_element_type=jnp.float32
        ).astype(jnp.bfloat16)
        for k in range(chunks)
    ]
    picked.append(jnp.pad(send_prob.T, ((0, 0), (0, LANES - slots)))[None])
    message = jnp.concatenate(picked, axis=0)
    message_rows = message.shape[0]
    message = message.transpose(1, 0, 2).reshape(rack_count, message_rows // 2, 2, LANES)
    lane = jnp.arange(LANES, dtype=jnp.int32)
    row_ids = jnp.where(lane < slots, jnp.arange(rack_count, dtype=jnp.int32)[:, None] + rack_count * lane, -1)
    own_ids = place // PAIR * own_rows + jnp.arange(own_rows, dtype=jnp.int32)
    message, w_gate, w_up, w_down, own_ids, row_ids = lax.optimization_barrier(
        (message, w_gate, w_up, w_down, own_ids, row_ids)
    )
    came = exchange(message, "rack")
    came = came.reshape(rack_count, message_rows, LANES).transpose(1, 0, 2)

    own_weights = jnp.concatenate([w_gate[0], w_up[0], w_down[0]], axis=1)
    other_weights = lax.ppermute(own_weights, "local", partners)
    weights = jnp.concatenate([own_weights, other_weights], axis=0)
    weight_gu, weight_down = weights[:, : 2 * hidden_units], weights[:, 2 * hidden_units :]
    depth = (wide + LANES - 1) // LANES * LANES
    filled = lax.optimization_barrier(
        jnp.concatenate(
            [
                jnp.pad(weight_gu, ((0, depth - wide), (0, 0))),
                jnp.pad(weight_down, ((depth - wide, 0), (0, 0))),
            ],
            axis=1,
        )
    )
    came_prob = came[message_rows - 1].astype(jnp.float32)
    own_prob = jnp.sum(jnp.where(own_ids[:, None, None] == row_ids, came_prob, 0.0), axis=(1, 2))
    own_prob, came = lax.optimization_barrier((own_prob, came))
    rows_both = unpack(came, slots)
    partial = project(rows_both, filled, 2 * hidden_units)
    parts = exchange(partial.reshape(team, own_rows, 3 * hidden_units), "local", teams)
    sums = jnp.sum(parts.astype(jnp.float32), axis=0)

    grad_gate, grad_up, scaled, statistic = activate(
        sums[:, :hidden_units], sums[:, hidden_units : 2 * hidden_units], sums[:, 2 * hidden_units :], own_prob
    )
    stat_lanes = jnp.broadcast_to(statistic.astype(jnp.bfloat16)[:, None], (own_rows, LANES))
    packed = jnp.concatenate([grad_gate, grad_up, stat_lanes], axis=1)
    grads_in = exchange(jnp.broadcast_to(packed[None], (team,) + packed.shape), "local", teams)
    grads_in = grads_in.reshape(row_total, 2 * hidden_units + LANES)
    stats_in = grads_in[:, 2 * hidden_units : 2 * hidden_units + 1]

    term = lax.dot_general(
        grads_in[:, : 2 * hidden_units],
        filled[:wide, : 2 * hidden_units],
        (((1,), (1,)), ((), ())),
        preferred_element_type=jnp.float32,
    ).astype(jnp.bfloat16)
    back = jnp.concatenate([term, jnp.broadcast_to(stats_in, (row_total, depth - wide))], axis=1)
    back = back.reshape(slots, rack_count, depth // LANES, LANES).transpose(1, 0, 2, 3)
    back, rows_both, grads_in, scaled = lax.optimization_barrier((back, rows_both, grads_in, scaled))
    came_terms = exchange(back, "rack").reshape(rack_count, slots, depth)

    def outer(rows, grads, first):
        return lax.dot_general(
            rows[:, first : first + width], grads, (((0,), (0,)), ((), ())), preferred_element_type=jnp.float32
        )

    rows_x, rows_dy = rows_both[:, :wide], rows_both[:, wide:]
    gate_up_in = grads_in[:, : 2 * hidden_units]
    send_gu = outer(rows_x, gate_up_in, width).astype(jnp.bfloat16)
    piece = 2 * SIDE * PAIR
    first_gu = lax.ppermute(send_gu[:piece], "local", partners)
    other_gu = lax.ppermute(send_gu[piece:], "local", partners)
    first_gu, scaled = lax.optimization_barrier((first_gu, scaled))
    came_gu = jnp.concatenate([first_gu, other_gu], axis=0).astype(jnp.float32)
    grad_gu = (outer(rows_x, gate_up_in, 0) + came_gu).astype(jnp.bfloat16)

    row, column = place // SIDE, place % SIDE
    across = [(i, i // SIDE * SIDE + SIDE - 1 - i % SIDE) for i in range(local_count)]
    two = jnp.concatenate([scaled, lax.ppermute(scaled, "local", across)], axis=0)
    sides = local_count // SIDE
    around = [
        lax.ppermute(two, "local", [(i, (i + SIDE * step) % local_count) for i in range(local_count)])
        for step in range(sides - 1, 0, -1)
    ]
    scaled_in = jnp.concatenate(around + [two], axis=0)
    rows_split = rows_dy.reshape(sides, PAIR, own_rows, wide)
    rows_split = jnp.where(column < PAIR, rows_split, rows_split[:, ::-1])
    turned = lax.dynamic_slice_in_dim(
        jnp.concatenate([rows_split, rows_split], axis=0), (row + 1) % sides, sides, 0
    ).reshape(row_total, wide)
    came_d = lax.ppermute(outer(turned, scaled_in, width).astype(jnp.bfloat16), "local", partners)
    grad_d = (outer(turned, scaled_in, 0) + came_d.astype(jnp.float32)).astype(jnp.bfloat16)

    token_sums = jnp.einsum("srt,rsd->dt", selector_bf, came_terms[..., :wide], preferred_element_type=jnp.float32)
    came_stat = came_terms[..., wide].astype(jnp.float32).T
    stat_token = jnp.sum(jnp.where(selector, came_stat[:, :, None], 0.0), axis=0)
    prob_sums = jnp.sum(jnp.where(member, stat_token.T[:, None, :], 0.0), axis=2).T
    tail = jnp.concatenate([token_sums[width:], prob_sums], axis=0).astype(jnp.bfloat16)
    came_tail = lax.ppermute(tail, "local", partners)
    token_cols, prob_cols = finish(token_sums[:width], prob_sums, came_tail)
    return (
        token_cols.T,
        prob_cols.T,
        grad_gu[None, :, :hidden_units],
        grad_gu[None, :, hidden_units:],
        grad_d[None],
    )


def solution(mesh):
    placed = (
        P("rack", "local"),
        P("rack", "local"),
        P("rack", None),
        P("rack", None),
        P("rack", "local", None),
        P("rack", "local", None),
        P("rack", "local", None),
    )
    return jax.shard_map(
        local,
        mesh=mesh,
        in_specs=placed,
        out_specs=(
            P("rack", "local"),
            P("rack", None),
            P("rack", "local", None),
            P("rack", "local", None),
            P("rack", "local", None),
        ),
        check_vma=False,
    )
```
